512 devices in a mesh: tm: 32 (over y, z_hi, core), space: 16 (over x, z_lo).
Axes of the slice: x: 4, y: 4, z: 16 (z_hi: 4, z_lo: 4; z = z_hi * 4 + z_lo), core: 2. Of those that a mesh axis runs over, the one named last changes fastest.
Arguments:
- queries: bfloat16 [65536, 4096], P(('tm', 'space')), may hold values from -8 to 8
- keys: bfloat16 [65536, 4096], P(('tm', 'space')), may hold values from -8 to 8
- values: bfloat16 [65536, 4096], P(('tm', 'space')), may hold values from -6 to 6
- tile_mask: int32 [512, 512], P('tm'), may hold values from 0 to 1, as said below
Outputs:
- attended: bfloat16 [65536, 4096], P(('tm', 'space'))
The draws below stay inside these ranges and needn't reach their ends.
Inputs may be any that keep to these rules, and one draw needn't show every extreme that they name: `tile_mask`: tile t holds tokens t * 128 to t * 128 + 127, of frame group t // 16 and height band t % 16. Every diagonal entry is 1. A query tile's ones lie in its own frame group or in the two adjacent ones. Each row has at most 15 ones, and some row exactly 15. For each frame group and each adjacent group that exists, the key tiles of the adjacent group that some query tile of the group uses number exactly 8.
All inputs are finite; a program needn't handle non-finite values.
Results may differ from the reference program's by a relative error of at most 0.0049.
Values may be sent and summed in bfloat16 or wider, within the bound.
A program may use at most 64 MiB of HBM per device.

```python
import math
import jax
import jax.numpy as jnp
from jax import lax

TILE = 128
HEADS = 32
HEAD_DIM = 128
REACH = 4
BANDS = 16
GROUPS = 32
TILES = 512
TOKENS = 65536
UMAX = 8
PICKS = 3
KMAX = 15


def draw_queries(key, part):
    key = jax.random.fold_in(key, 1)
    drawn = jax.random.truncated_normal(key, -6.0, 6.0, (TOKENS, HEADS * HEAD_DIM), jnp.float32)
    return drawn.astype(jnp.bfloat16)


def draw_keys(key, part):
    key = jax.random.fold_in(key, 2)
    drawn = jax.random.truncated_normal(key, -6.0, 6.0, (TOKENS, HEADS * HEAD_DIM), jnp.float32)
    return drawn.astype(jnp.bfloat16)


def draw_tile_mask(key, part):
    key = jax.random.fold_in(key, 3)
    reach_key, prior_key, next_key, perm_key = jax.random.split(key, 4)
    tile_ids = jnp.arange(TILES, dtype=jnp.int32)
    group_of = tile_ids // BANDS
    band_of = tile_ids % BANDS
    forced = tile_ids == GROUPS // 2 * BANDS + BANDS // 2
    reach_len = jnp.where(forced, REACH, jax.random.randint(reach_key, (TILES,), 1, REACH + 1))
    prior_count = jnp.where(forced, PICKS, jax.random.randint(prior_key, (TILES,), 1, PICKS + 1))
    next_count = jnp.where(forced, PICKS, jax.random.randint(next_key, (TILES,), 1, PICKS + 1))
    perm_keys = jax.random.split(perm_key, 2 * GROUPS)
    orders = jax.vmap(lambda one_key: jax.random.permutation(one_key, BANDS))(perm_keys)
    chosen_bands = orders[:, :UMAX].reshape(2, GROUPS, UMAX).astype(jnp.int32)
    column_group = group_of[None, :]
    column_band = band_of[None, :]
    marked = (column_group == group_of[:, None]) & (jnp.abs(column_band - band_of[:, None]) <= reach_len[:, None])
    for offset in range(PICKS):
        slot_pos = (band_of + offset) % UMAX
        prior_band = chosen_bands[0, group_of, slot_pos]
        next_band = chosen_bands[1, group_of, slot_pos]
        marked = marked | (column_group == group_of[:, None] - 1) & (column_band == prior_band[:, None]) & (offset < prior_count)[:, None]
        marked = marked | (column_group == group_of[:, None] + 1) & (column_band == next_band[:, None]) & (offset < next_count)[:, None]
    return marked.astype(jnp.int32)


def shard_levels(stream_key, shape, cuts, low, top_value):
    factor_of, own = 1.0, jax.random.fold_in(stream_key, 6)
    for dim, blocks in cuts:
        heights = jnp.exp(jax.random.uniform(jax.random.fold_in(own, dim), (blocks,), jnp.float32, low / len(cuts), top_value / len(cuts)))
        factor_of = factor_of * jnp.repeat(heights, shape[dim] // blocks).reshape([-1 if axis == dim else 1 for axis in range(len(shape))])
    return factor_of


def gaussian(own_key, shape, deviation, most, cuts=(), held_as=jnp.bfloat16):
    values = jax.random.normal(own_key, shape, jnp.float32) * deviation
    if len(cuts) > 0:
        values = shard_levels(own_key, shape, cuts, -0.22, 0.18) * values
    return jnp.clip(values, min=-most, max=most).astype(held_as)


def setup_inputs(seed: int = 0) -> dict:
    splits = jax.random.split(jax.random.key(seed), 5)
    queries = draw_queries(jax.random.fold_in(splits[4], 71), 0)
    keys = draw_keys(jax.random.fold_in(splits[4], 71), 0)
    values = gaussian(splits[2], (TOKENS, HEADS * HEAD_DIM), 1.0, 6.0, ((0, 512),))
    tile_mask = draw_tile_mask(jax.random.fold_in(splits[4], 71), 0)
    return {"queries": queries, "keys": keys, "values": values, "tile_mask": tile_mask}


def reference(queries, keys, values, tile_mask):
    inv_root = 1.0 / math.sqrt(HEAD_DIM)
    query_tiles = queries.reshape(TILES, TILE, HEADS, HEAD_DIM)
    key_tiles = keys.reshape(TILES, TILE, HEADS, HEAD_DIM)
    value_tiles = values.reshape(TILES, TILE, HEADS, HEAD_DIM)

    def one_tile(tile_index):
        mask_row = tile_mask[tile_index]
        chosen = jnp.argsort(1 - mask_row, stable=True)[:KMAX].astype(jnp.int32)
        usable = jnp.arange(KMAX, dtype=jnp.int32) < jnp.sum(mask_row)
        key_rows = key_tiles[chosen].reshape(KMAX * TILE, HEADS, HEAD_DIM).astype(jnp.float32)
        value_rows = value_tiles[chosen].reshape(KMAX * TILE, HEADS, HEAD_DIM).astype(jnp.float32)
        key_live = jnp.repeat(usable, TILE)
        scores = jnp.einsum('qhd,khd->hqk', query_tiles[tile_index].astype(jnp.float32), key_rows) * inv_root
        scores = jnp.where(key_live[None, None, :], scores, -jnp.inf)
        row_top = lax.optimization_barrier(jnp.max(scores, axis=2, keepdims=True))
        raised = jnp.exp(scores - row_top)
        weights = (raised / lax.optimization_barrier(jnp.sum(raised, axis=2, keepdims=True))).astype(jnp.bfloat16)
        output = jnp.einsum('hqk,khd->qhd', weights.astype(jnp.float32), value_rows)
        return output.astype(jnp.bfloat16)
    result = lax.map(one_tile, jnp.arange(TILES, dtype=jnp.int32))
    return result.reshape(TOKENS, HEADS * HEAD_DIM)
```

```python
import functools
import math

import jax
import jax.numpy as jnp
from jax import lax
from jax.experimental import pallas as pl
from jax.experimental.pallas import tpu as pltpu
from jax.sharding import PartitionSpec as P

HEAD_DIM = 128
REACH = 4
UMAX = 8
PICKS = 3
MASKED = -1e30
MESH = pl.DeviceIdType.MESH


def adjacent(tile_mask, group, bands, exists):
    block = lax.dynamic_slice(tile_mask, (0, group * bands), (bands, bands))
    block = jnp.where(exists, block, 0)
    ids = jnp.arange(bands, dtype=jnp.int32)
    upto = (ids[:, None] <= ids[None, :]).astype(jnp.int32)
    used = jnp.max(block, axis=0)
    place = jnp.sum(used[:, None] * upto, axis=0) - 1
    slots = jnp.arange(UMAX, dtype=jnp.int32)
    hit = (used[:, None] > 0) & (place[:, None] == slots[None, :])
    tiles = jnp.sum(jnp.where(hit, ids[:, None], 0), axis=0)
    order = jnp.sum(block[:, :, None] * upto[None], axis=1) - 1
    wanted = jnp.arange(PICKS, dtype=jnp.int32)
    taken = (block[:, :, None] > 0) & (order[:, :, None] == wanted)
    picks = jnp.sum(jnp.where(taken, place[None, :, None], 0), axis=1)
    live = jnp.sum(taken.astype(jnp.int32), axis=1)
    return tiles, picks, live


def kernel(
    bands, groups, heads,
    meta, lists, q_in, k_in, v_in, out,
    *scratch,
):
    q_all, k_all, v_all, o_all = (scratch[i * heads : (i + 1) * heads] for i in range(4))
    halo_out = [scratch[(4 + i) * heads : (5 + i) * heads] for i in range(2)]
    halo_in = [scratch[(6 + i) * heads : (7 + i) * heads] for i in range(2)]
    (own_sem, send_sem, recv_sem, halo_send, halo_recv, o_own, o_send, o_recv) = scratch[8 * heads :]
    g = lax.axis_index("tm")
    me = lax.axis_index("space")
    tile = q_in.shape[0]
    window = min(2 * REACH + 1, bands)

    barrier = pltpu.get_barrier_semaphore()

    @pl.loop(1, bands)
    def _(d):
        pl.semaphore_signal(barrier, inc=1, device_id={"space": lax.rem(me + d, bands)}, device_id_type=MESH)

    for step in (1, groups - 1):
        pl.semaphore_signal(barrier, inc=1, device_id={"tm": lax.rem(g + step, groups)}, device_id_type=MESH)

    def own_copies():
        found = []
        for a, (source, target) in enumerate(((k_in, k_all), (v_in, v_all), (q_in, q_all))):
            for h in range(heads):
                columns = pl.ds(pl.multiple_of((me * heads + h) * HEAD_DIM, HEAD_DIM), HEAD_DIM)
                found.append(pltpu.make_async_copy(source.at[:, columns], target[h].at[me], own_sem.at[a, h]))
        return found

    for copy in own_copies():
        copy.start()

    pl.semaphore_wait(barrier, bands + 1)

    def spread(a, h, peer, source_band):
        source, target = ((k_in, k_all), (v_in, v_all), (q_in, q_all))[a]
        columns = pl.ds(pl.multiple_of((peer * heads + h) * HEAD_DIM, HEAD_DIM), HEAD_DIM)
        return pltpu.make_async_remote_copy(
            src_ref=source.at[:, columns],
            dst_ref=target[h].at[source_band],
            send_sem=send_sem.at[a, h, peer],
            recv_sem=recv_sem.at[a, h, source_band],
            device_id={"space": peer},
            device_id_type=MESH,
        )

    def start_spread(a, h):
        @pl.loop(1, bands)
        def _(d):
            peer = lax.rem(me + d, bands)
            spread(a, h, peer, me).start()

    def wait_spread(a, h):
        @pl.loop(1, bands)
        def _(d):
            peer = lax.rem(me + d, bands)
            spread(a, h, peer, peer).wait_recv()

    for a, h in [(0, 0), (1, 0), (0, 1), (1, 1), (2, 0), (2, 1)][: 3 * heads]:
        start_spread(a, h)
    for copy in own_copies():
        copy.wait()

    def halo(side, h):
        return pltpu.make_async_remote_copy(
            src_ref=halo_out[side][h],
            dst_ref=halo_in[side][h],
            send_sem=halo_send.at[side, h],
            recv_sem=halo_recv.at[side, h],
            device_id={"tm": g + 1 if side == 0 else g - 1},
            device_id_type=MESH,
        )

    sends = (g < groups - 1, g > 0)
    receives = (g > 0, g < groups - 1)

    for h in range(heads):
        wait_spread(0, h)
        wait_spread(1, h)
        for side in range(2):
            @pl.when(sends[side])
            def _():
                for s in range(UMAX):
                    index = lists[side, s]
                    halo_out[side][h][0, s] = k_all[h][index]
                    halo_out[side][h][1, s] = v_all[h][index]
                halo(side, h).start()

    for side in range(2):
        @pl.when(jnp.logical_not(receives[side]))
        def _():
            for h in range(heads):
                halo_in[side][h][...] = jnp.zeros(halo_in[side][h].shape, halo_in[side][h].dtype)

    scale = math.log2(math.e) / math.sqrt(HEAD_DIM)
    across = (((1,), (1,)), ((), ()))

    def attend(h, r):
        query = q_all[h][r]
        first = jnp.clip(r - REACH, 0, bands - window)
        near = k_all[h][pl.ds(first, window)].reshape(window * tile, HEAD_DIM)
        scores = lax.dot_general(query, near, across, preferred_element_type=jnp.float32)
        parts, value_parts = [], []
        for j in range(window):
            bias = jnp.where(meta[r, first + j] > 0, 0.0, MASKED)
            parts.append(scores[:, j * tile : (j + 1) * tile] + bias)
        for side in range(2):
            for p in range(PICKS):
                at = bands + 2 * PICKS * side + p
                index = meta[r, at]
                bias = jnp.where(meta[r, at + PICKS] > 0, 0.0, MASKED)
                one = lax.dot_general(query, halo_in[side][h][0, index], across, preferred_element_type=jnp.float32)
                parts.append(one + bias)
                value_parts.append((side, index))
        top = functools.reduce(jnp.maximum, parts)
        top = jnp.max(top, axis=1, keepdims=True)
        raised = [jnp.exp2((part - top) * scale) for part in parts]
        total = jnp.sum(functools.reduce(jnp.add, raised), axis=1, keepdims=True)
        raised = [one.astype(jnp.bfloat16) for one in raised]
        near = v_all[h][pl.ds(first, window)].reshape(window * tile, HEAD_DIM)
        result = jnp.dot(jnp.concatenate(raised[:window], axis=1), near, preferred_element_type=jnp.float32)
        for one, (side, index) in zip(raised[window:], value_parts):
            result = result + jnp.dot(one, halo_in[side][h][1, index], preferred_element_type=jnp.float32)
        o_all[h][r] = (result / total).astype(o_all[h].dtype)

    def give_back(h, peer, head_group):
        columns = pl.ds(pl.multiple_of((head_group * heads + h) * HEAD_DIM, HEAD_DIM), HEAD_DIM)
        return pltpu.make_async_remote_copy(
            src_ref=o_all[h].at[peer],
            dst_ref=out.at[:, columns],
            send_sem=o_send.at[h, peer],
            recv_sem=o_recv.at[h, head_group],
            device_id={"space": peer},
            device_id_type=MESH,
        )

    def keep(h):
        columns = pl.ds(pl.multiple_of((me * heads + h) * HEAD_DIM, HEAD_DIM), HEAD_DIM)
        return pltpu.make_async_copy(o_all[h].at[me], out.at[:, columns], o_own.at[h])

    for h in range(heads):
        wait_spread(2, h)
        for side in range(2):
            @pl.when(receives[side])
            def _():
                halo(side, h).wait_recv()

        @pl.loop(0, bands)
        def _(r):
            attend(h, r)

        @pl.loop(1, bands)
        def _(d):
            give_back(h, lax.rem(me + d, bands), me).start()

        keep(h).start()

    for h in range(heads):
        for a in range(3):
            @pl.loop(1, bands)
            def _(d):
                peer = lax.rem(me + d, bands)
                spread(a, h, peer, me).wait_send()

        for side in range(2):
            @pl.when(sends[side])
            def _():
                halo(side, h).wait_send()

        @pl.loop(1, bands)
        def _(d):
            peer = lax.rem(me + d, bands)
            give_back(h, peer, me).wait_send()
            give_back(h, peer, peer).wait_recv()

        keep(h).wait()


def body(queries, keys, values, tile_mask):
    bands = lax.axis_size("space")
    groups = lax.axis_size("tm")
    g = lax.axis_index("tm")
    tile, width = queries.shape
    heads = width // HEAD_DIM // bands
    own = lax.dynamic_slice(tile_mask, (0, g * bands), (bands, bands))
    prior_tiles, prior_picks, prior_live = adjacent(tile_mask, jnp.maximum(g - 1, 0), bands, g > 0)
    next_tiles, next_picks, next_live = adjacent(tile_mask, jnp.minimum(g + 1, groups - 1), bands, g < groups - 1)
    meta = jnp.concatenate([own, prior_picks, prior_live, next_picks, next_live], axis=1)
    for_next = lax.ppermute(prior_tiles, "tm", [(i + 1, i) for i in range(groups - 1)])
    for_prior = lax.ppermute(next_tiles, "tm", [(i, i + 1) for i in range(groups - 1)])
    lists = jnp.stack([for_next, for_prior])
    whole = (bands, tile, HEAD_DIM)
    halo = (2, UMAX, tile, HEAD_DIM)
    dma = pltpu.SemaphoreType.DMA
    return pl.pallas_call(
        functools.partial(kernel, bands, groups, heads),
        out_shape=jax.ShapeDtypeStruct((tile, width), jnp.bfloat16),
        in_specs=[pl.BlockSpec(memory_space=pltpu.SMEM)] * 2 + [pl.BlockSpec(memory_space=pl.ANY)] * 3,
        out_specs=pl.BlockSpec(memory_space=pl.ANY),
        scratch_shapes=[pltpu.VMEM(whole, jnp.bfloat16)] * (4 * heads)
        + [pltpu.VMEM(halo, jnp.bfloat16)] * (4 * heads)
        + [
            dma((3, heads)),
            dma((3, heads, bands)),
            dma((3, heads, bands)),
            dma((2, heads)),
            dma((2, heads)),
            dma((heads,)),
            dma((heads, bands)),
            dma((heads, bands)),
        ],
        compiler_params=pltpu.CompilerParams(
            collective_id=0, has_side_effects=True, vmem_limit_bytes=40 * 1024 * 1024
        ),
    )(meta, lists, queries, keys, values)


def solution(mesh):
    placed = (
        P(("tm", "space"), None),
        P(("tm", "space"), None),
        P(("tm", "space"), None),
        P("tm", None),
    )
    return jax.shard_map(
        body, mesh=mesh, in_specs=placed, out_specs=P(("tm", "space"), None), check_vma=False
    )
```

```python
import functools
import math

import jax
import jax.numpy as jnp
from jax import lax
from jax.experimental import pallas as pl
from jax.experimental.pallas import tpu as pltpu
from jax.sharding import PartitionSpec as P

HEAD_DIM = 128
REACH = 4
UMAX = 8
PICKS = 3
MASKED = -1e30
MESH = pl.DeviceIdType.MESH


def adjacent(tile_mask, group, bands, exists):
    block = lax.dynamic_slice(tile_mask, (0, group * bands), (bands, bands))
    block = jnp.where(exists, block, 0)
    ids = jnp.arange(bands, dtype=jnp.int32)
    upto = (ids[:, None] <= ids[None, :]).astype(jnp.int32)
    used = jnp.max(block, axis=0)
    place = jnp.sum(used[:, None] * upto, axis=0) - 1
    slots = jnp.arange(UMAX, dtype=jnp.int32)
    hit = (used[:, None] > 0) & (place[:, None] == slots[None, :])
    tiles = jnp.sum(jnp.where(hit, ids[:, None], 0), axis=0)
    order = jnp.sum(block[:, :, None] * upto[None], axis=1) - 1
    wanted = jnp.arange(PICKS, dtype=jnp.int32)
    taken = (block[:, :, None] > 0) & (order[:, :, None] == wanted)
    picks = jnp.sum(jnp.where(taken, place[None, :, None], 0), axis=1)
    live = jnp.sum(taken.astype(jnp.int32), axis=1)
    return tiles, picks, live


def kernel(
    bands, groups, heads,
    meta, wants, q_in, k_in, v_in, out,
    *scratch,
):
    q_all, k_all, v_all, o_all = (scratch[i * heads : (i + 1) * heads] for i in range(4))
    halo_out = [scratch[(4 + i) * heads : (5 + i) * heads] for i in range(2)]
    halo_in = [scratch[(6 + i) * heads : (7 + i) * heads] for i in range(2)]
    near_sum, near_top, near_total = (scratch[(8 + i) * heads : (9 + i) * heads] for i in range(3))
    (
        asked, lists, ask_send, ask_recv, ask_own,
        own_sem, send_sem, recv_sem, halo_send, halo_recv, o_own, o_send, o_recv,
    ) = scratch[11 * heads :]
    g = lax.axis_index("tm")
    me = lax.axis_index("space")
    tile = q_in.shape[0]
    window = min(2 * REACH + 1, bands)

    barrier = pltpu.get_barrier_semaphore()

    @pl.loop(1, bands)
    def _(d):
        pl.semaphore_signal(barrier, inc=1, device_id={"space": lax.rem(me + d, bands)}, device_id_type=MESH)

    for step in (1, groups - 1):
        pl.semaphore_signal(barrier, inc=1, device_id={"tm": lax.rem(g + step, groups)}, device_id_type=MESH)

    def own_copies():
        found = []
        for a, (source, target) in enumerate(((k_in, k_all), (v_in, v_all), (q_in, q_all))):
            for h in range(heads):
                columns = pl.ds(pl.multiple_of((me * heads + h) * HEAD_DIM, HEAD_DIM), HEAD_DIM)
                found.append(pltpu.make_async_copy(source.at[:, columns], target[h].at[me], own_sem.at[a, h]))
        return found

    for copy in own_copies():
        copy.start()

    pl.semaphore_wait(barrier, bands + 1)

    exists = (g < groups - 1, g > 0)

    def ask(side):
        return pltpu.make_async_remote_copy(
            src_ref=wants.at[side],
            dst_ref=asked[1 - side],
            send_sem=ask_send.at[side],
            recv_sem=ask_recv.at[1 - side],
            device_id={"tm": g + 1 if side == 0 else g - 1},
            device_id_type=MESH,
        )

    for side in range(2):
        @pl.when(exists[side])
        def _():
            ask(side).start()

    def spread(a, h, peer, source_band):
        source, target = ((k_in, k_all), (v_in, v_all), (q_in, q_all))[a]
        columns = pl.ds(pl.multiple_of((peer * heads + h) * HEAD_DIM, HEAD_DIM), HEAD_DIM)
        return pltpu.make_async_remote_copy(
            src_ref=source.at[:, columns],
            dst_ref=target[h].at[source_band],
            send_sem=send_sem.at[a, h, peer],
            recv_sem=recv_sem.at[a, h, source_band],
            device_id={"space": peer},
            device_id_type=MESH,
        )

    def start_spread(a, h):
        @pl.loop(1, bands)
        def _(d):
            peer = lax.rem(me + d, bands)
            spread(a, h, peer, me).start()

    def wait_spread(a, h):
        @pl.loop(1, bands)
        def _(d):
            peer = lax.rem(me + d, bands)
            spread(a, h, peer, peer).wait_recv()

    for a, h in [(0, 0), (1, 0), (0, 1), (1, 1), (2, 0), (2, 1)][: 3 * heads]:
        start_spread(a, h)
    for copy in own_copies():
        copy.wait()

    def halo(side, h):
        return pltpu.make_async_remote_copy(
            src_ref=halo_out[side][h],
            dst_ref=halo_in[side][h],
            send_sem=halo_send.at[side, h],
            recv_sem=halo_recv.at[side, h],
            device_id={"tm": g + 1 if side == 0 else g - 1},
            device_id_type=MESH,
        )

    def fetch_list(side):
        return pltpu.make_async_copy(asked[side], lists[side], ask_own.at[side])

    for side in range(2):
        @pl.when(exists[side])
        def _():
            ask(1 - side).wait_recv()
            fetch_list(side).start()
            fetch_list(side).wait()

    for h in range(heads):
        wait_spread(0, h)
        wait_spread(1, h)
        for side in range(2):
            @pl.when(exists[side])
            def _():
                for s in range(UMAX):
                    index = lists[side][0, s]
                    halo_out[side][h][0, s] = k_all[h][index]
                    halo_out[side][h][1, s] = v_all[h][index]
                halo(side, h).start()

    for side in range(2):
        @pl.when(jnp.logical_not(exists[1 - side]))
        def _():
            for h in range(heads):
                halo_in[side][h][...] = jnp.zeros(halo_in[side][h].shape, halo_in[side][h].dtype)

    scale = math.log2(math.e) / math.sqrt(HEAD_DIM)
    across = (((1,), (1,)), ((), ()))

    def softmax(parts, floor=None):
        top = jnp.max(functools.reduce(jnp.maximum, parts), axis=1, keepdims=True)
        if floor is not None:
            top = jnp.maximum(top, floor)
        raised = [jnp.exp2((part - top) * scale) for part in parts]
        total = jnp.sum(functools.reduce(jnp.add, raised), axis=1, keepdims=True)
        return top, total, [one.astype(jnp.bfloat16) for one in raised]

    def attend_near(h, r):
        first = jnp.clip(r - REACH, 0, bands - window)
        near = k_all[h][pl.ds(first, window)].reshape(window * tile, HEAD_DIM)
        scores = lax.dot_general(q_all[h][r], near, across, preferred_element_type=jnp.float32)
        parts = [
            scores[:, j * tile : (j + 1) * tile] + jnp.where(meta[r, first + j] > 0, 0.0, MASKED)
            for j in range(window)
        ]
        top, total, raised = softmax(parts)
        near = v_all[h][pl.ds(first, window)].reshape(window * tile, HEAD_DIM)
        near_sum[h][r] = jnp.dot(jnp.concatenate(raised, axis=1), near, preferred_element_type=jnp.float32)
        near_top[h][r] = jnp.broadcast_to(top, (tile, HEAD_DIM))
        near_total[h][r] = jnp.broadcast_to(total, (tile, HEAD_DIM))

    def attend_far(h, r):
        key_parts, value_parts, biases = [], [], []
        for side in range(2):
            for p in range(PICKS):
                at = bands + 2 * PICKS * side + p
                index = meta[r, at]
                biases.append(jnp.where(meta[r, at + PICKS] > 0, 0.0, MASKED))
                key_parts.append(halo_in[side][h][0, index])
                value_parts.append(halo_in[side][h][1, index])
        far = jnp.concatenate(key_parts, axis=0)
        scores = lax.dot_general(q_all[h][r], far, across, preferred_element_type=jnp.float32)
        parts = [scores[:, j * tile : (j + 1) * tile] + bias for j, bias in enumerate(biases)]
        before = near_top[h][r][:, :1]
        top, total, raised = softmax(parts, before)
        kept = jnp.exp2((before - top) * scale)
        total = near_total[h][r][:, :1] * kept + total
        far = jnp.concatenate(value_parts, axis=0)
        result = jnp.dot(jnp.concatenate(raised, axis=1), far, preferred_element_type=jnp.float32)
        o_all[h][r] = ((near_sum[h][r] * kept + result) / total).astype(o_all[h].dtype)

    def give_back(h, peer, head_group):
        columns = pl.ds(pl.multiple_of((head_group * heads + h) * HEAD_DIM, HEAD_DIM), HEAD_DIM)
        return pltpu.make_async_remote_copy(
            src_ref=o_all[h].at[peer],
            dst_ref=out.at[:, columns],
            send_sem=o_send.at[h, peer],
            recv_sem=o_recv.at[h, head_group],
            device_id={"space": peer},
            device_id_type=MESH,
        )

    def keep(h):
        columns = pl.ds(pl.multiple_of((me * heads + h) * HEAD_DIM, HEAD_DIM), HEAD_DIM)
        return pltpu.make_async_copy(o_all[h].at[me], out.at[:, columns], o_own.at[h])

    for h in range(heads):
        wait_spread(2, h)

        @pl.loop(0, bands, unroll=2)
        def _(r):
            attend_near(h, r)

    for h in range(heads):
        for side in range(2):
            @pl.when(exists[1 - side])
            def _():
                halo(side, h).wait_recv()

        @pl.loop(0, bands // 2)
        def _(i):
            places = [lax.rem(me + 2 * i + j + 1, bands) for j in range(2)]
            for r in places:
                attend_far(h, r)
            give_back(h, places[0], me).start()

            @pl.when(i < bands // 2 - 1)
            def _():
                give_back(h, places[1], me).start()

        keep(h).start()

    for h in range(heads):
        for a in range(3):
            @pl.loop(1, bands)
            def _(d):
                peer = lax.rem(me + d, bands)
                spread(a, h, peer, me).wait_send()

        for side in range(2):
            @pl.when(exists[side])
            def _():
                halo(side, h).wait_send()
                if h == 0:
                    ask(side).wait_send()

        @pl.loop(1, bands)
        def _(d):
            peer = lax.rem(me + d, bands)
            give_back(h, peer, me).wait_send()
            give_back(h, peer, peer).wait_recv()

        keep(h).wait()


def body(queries, keys, values, tile_mask):
    bands = lax.axis_size("space")
    groups = lax.axis_size("tm")
    g = lax.axis_index("tm")
    tile, width = queries.shape
    heads = width // HEAD_DIM // bands
    own = lax.dynamic_slice(tile_mask, (0, g * bands), (bands, bands))
    prior_tiles, prior_picks, prior_live = adjacent(tile_mask, jnp.maximum(g - 1, 0), bands, g > 0)
    next_tiles, next_picks, next_live = adjacent(tile_mask, jnp.minimum(g + 1, groups - 1), bands, g < groups - 1)
    meta = jnp.concatenate([own, prior_picks, prior_live, next_picks, next_live], axis=1)
    wants = jnp.zeros((2, 8, 128), jnp.int32).at[:, 0, :UMAX].set(jnp.stack([next_tiles, prior_tiles]))
    whole = (bands, tile, HEAD_DIM)
    halo = (2, UMAX, tile, HEAD_DIM)
    dma = pltpu.SemaphoreType.DMA
    return pl.pallas_call(
        functools.partial(kernel, bands, groups, heads),
        out_shape=jax.ShapeDtypeStruct((tile, width), jnp.bfloat16),
        in_specs=[pl.BlockSpec(memory_space=pltpu.SMEM), pl.BlockSpec(memory_space=pltpu.VMEM)]
        + [pl.BlockSpec(memory_space=pl.ANY)] * 3,
        out_specs=pl.BlockSpec(memory_space=pl.ANY),
        scratch_shapes=[pltpu.VMEM(whole, jnp.bfloat16)] * (4 * heads)
        + [pltpu.VMEM(halo, jnp.bfloat16)] * (4 * heads)
        + [pltpu.VMEM(whole, jnp.float32)] * (3 * heads)
        + [[pltpu.VMEM((8, 128), jnp.int32)] * 2, [pltpu.SMEM((8, 128), jnp.int32)] * 2]
        + [
            dma((2,)),
            dma((2,)),
            dma((2,)),
            dma((3, heads)),
            dma((3, heads, bands)),
            dma((3, heads, bands)),
            dma((2, heads)),
            dma((2, heads)),
            dma((heads,)),
            dma((heads, bands)),
            dma((heads, bands)),
        ],
        compiler_params=pltpu.CompilerParams(
            collective_id=0, has_side_effects=True, vmem_limit_bytes=56 * 1024 * 1024
        ),
    )(meta, wants, queries, keys, values)


def solution(mesh):
    placed = (
        P(("tm", "space"), None),
        P(("tm", "space"), None),
        P(("tm", "space"), None),
        P("tm", None),
    )
    return jax.shard_map(
        body, mesh=mesh, in_specs=placed, out_specs=P(("tm", "space"), None), check_vma=False
    )
```

```python
import functools
import math

import jax
import jax.numpy as jnp
from jax import lax
from jax.experimental import pallas as pl
from jax.experimental.pallas import tpu as pltpu
from jax.sharding import PartitionSpec as P

HEAD_DIM = 128
REACH = 4
UMAX = 8
PICKS = 3
LANES = 128
MASKED = -1e30
MESH = pl.DeviceIdType.MESH


def plan(mask, g, bands):
    total = mask.shape[1]
    near = pltpu.roll(mask, lax.rem(2 * total - (g - 1) * bands, total), 1)[:, :LANES]
    lane = lax.broadcasted_iota(jnp.int32, near.shape, 1)
    list_lane = lax.broadcasted_iota(jnp.int32, (8, LANES), 1)
    used = jnp.max(near, axis=0, keepdims=True)
    packed = jnp.where(lane < 3 * bands, near, 0)
    lists = []
    for side, base in enumerate((2 * bands, 0)):
        place = jnp.zeros((1, LANES), jnp.int32)
        order = jnp.zeros_like(near)
        picks = [jnp.zeros_like(near) for _ in range(PICKS)]
        tiles = jnp.zeros((8, LANES), jnp.int32)
        for c in range(bands):
            taken = jnp.broadcast_to(near[:, base + c : base + c + 1], near.shape)
            wanted = jnp.broadcast_to(used[:, base + c : base + c + 1], (1, LANES))
            tiles = tiles + jnp.where((wanted > 0) & (list_lane == place), c, 0)
            for p in range(PICKS):
                picks[p] = picks[p] + jnp.where((taken > 0) & (order == p), place, 0)
            place = place + wanted
            order = order + taken
        at = 3 * bands + 2 * PICKS * side
        for p in range(PICKS):
            packed = jnp.where(lane == at + p, picks[p], packed)
            packed = jnp.where(lane == at + PICKS + p, jnp.where(order > p, 1, 0), packed)
        lists.append(tiles)
    return packed, lists


def kernel(bands, groups, heads, mask_in, q_in, k_in, v_in, out, *scratch):
    q_all, k_all, v_all, o_all = (scratch[i * heads : (i + 1) * heads] for i in range(4))
    halo_out = [scratch[(4 + i) * heads : (5 + i) * heads] for i in range(2)]
    halo_in = [scratch[(6 + i) * heads : (7 + i) * heads] for i in range(2)]
    near_sum, near_top, near_total = (scratch[(8 + i) * heads : (9 + i) * heads] for i in range(3))
    (
        mask, packed, meta, wants, asked, lists,
        mask_sem, meta_sem, ask_send, ask_recv, ask_own,
        own_sem, send_sem, recv_sem, halo_send, halo_recv, o_own, o_send, o_recv,
    ) = scratch[11 * heads :]
    g = lax.axis_index("tm")
    me = lax.axis_index("space")
    tile = q_in.shape[0]
    window = min(2 * REACH + 1, bands)
    exists = (g < groups - 1, g > 0)
    moved = ((k_in, k_all), (v_in, v_all), (q_in, q_all))

    barrier = pltpu.get_barrier_semaphore()

    @pl.loop(1, bands)
    def _(d):
        pl.semaphore_signal(barrier, inc=1, device_id={"space": lax.rem(me + d, bands)}, device_id_type=MESH)

    for step in (1, groups - 1):
        pl.semaphore_signal(barrier, inc=1, device_id={"tm": lax.rem(g + step, groups)}, device_id_type=MESH)

    def head_columns(owner, h):
        return pl.ds(pl.multiple_of((owner * heads + h) * HEAD_DIM, HEAD_DIM), HEAD_DIM)

    fetch_mask = pltpu.make_async_copy(mask_in, mask, mask_sem)
    fetch_mask.start()

    def own_copy(a, h):
        source, target = moved[a]
        return pltpu.make_async_copy(source.at[:, head_columns(me, h)], target[h].at[me], own_sem.at[a, h])

    for h in range(heads):
        for a in range(3):
            own_copy(a, h).start()

    fetch_mask.wait()
    packed[...], found = plan(mask[...], g, bands)
    for side in range(2):
        wants[side][...] = found[side]
    fetch_meta = pltpu.make_async_copy(packed, meta, meta_sem)
    fetch_meta.start()

    pl.semaphore_wait(barrier, bands + 1)

    def ask(side):
        return pltpu.make_async_remote_copy(
            src_ref=wants[side],
            dst_ref=asked[1 - side],
            send_sem=ask_send.at[side],
            recv_sem=ask_recv.at[1 - side],
            device_id={"tm": g + 1 if side == 0 else g - 1},
            device_id_type=MESH,
        )

    for side in range(2):
        @pl.when(exists[side])
        def _():
            ask(side).start()

    def spread(a, h, peer):
        source, target = moved[a]
        return pltpu.make_async_remote_copy(
            src_ref=source.at[:, head_columns(peer, h)],
            dst_ref=target[h].at[me],
            send_sem=send_sem.at[a, h],
            recv_sem=recv_sem.at[a, h],
            device_id={"space": peer},
            device_id_type=MESH,
        )

    def start_spread(a, h):
        @pl.loop(1, bands)
        def _(d):
            spread(a, h, lax.rem(me + d, bands)).start()

    def wait_bytes(buffer, sem):
        part = buffer.at[pl.ds(0, bands - 1)]
        pltpu.make_async_copy(part, part, sem).wait()

    def wait_spread(a, h):
        wait_bytes(moved[a][1][h], recv_sem.at[a, h])
        own_copy(a, h).wait()

    for a, h in [(a, h) for h in range(heads) for a in (0, 1)] + [(2, h) for h in range(heads)]:
        start_spread(a, h)

    def halo(side, h):
        return pltpu.make_async_remote_copy(
            src_ref=halo_out[side][h],
            dst_ref=halo_in[side][h],
            send_sem=halo_send.at[side, h],
            recv_sem=halo_recv.at[side, h],
            device_id={"tm": g + 1 if side == 0 else g - 1},
            device_id_type=MESH,
        )

    def fetch_list(side):
        return pltpu.make_async_copy(asked[side], lists[side], ask_own.at[side])

    for side in range(2):
        @pl.when(jnp.logical_not(exists[1 - side]))
        def _():
            for h in range(heads):
                halo_in[side][h][...] = jnp.zeros(halo_in[side][h].shape, halo_in[side][h].dtype)

    fetch_meta.wait()
    for side in range(2):
        @pl.when(exists[side])
        def _():
            ask(1 - side).wait_recv()
            fetch_list(side).start()

    for side in range(2):
        @pl.when(exists[side])
        def _():
            fetch_list(side).wait()

    def fill_halo(h):
        wait_spread(0, h)
        wait_spread(1, h)
        for side in range(2):
            @pl.when(exists[side])
            def _():
                for s in range(UMAX):
                    index = lists[side][0, s]
                    halo_out[side][h][0, s] = k_all[h][index]
                    halo_out[side][h][1, s] = v_all[h][index]

    def each_side(action, h, receive=False):
        for side in range(2):
            @pl.when(exists[1 - side if receive else side])
            def _():
                action(halo(side, h))

    scale = math.log2(math.e) / math.sqrt(HEAD_DIM)
    across = (((1,), (1,)), ((), ()))

    def softmax(parts, floor=None):
        top = jnp.max(functools.reduce(jnp.maximum, parts), axis=1, keepdims=True)
        if floor is not None:
            top = jnp.maximum(top, floor)
        raised = [jnp.exp2((part - top) * scale) for part in parts]
        total = jnp.sum(functools.reduce(jnp.add, raised), axis=1, keepdims=True)
        return top, total, [one.astype(jnp.bfloat16) for one in raised]

    def attend_near(h, r):
        first = jnp.clip(r - REACH, 0, bands - window)
        near = k_all[h][pl.ds(first, window)].reshape(window * tile, HEAD_DIM)
        scores = lax.dot_general(q_all[h][r], near, across, preferred_element_type=jnp.float32)
        parts = [
            scores[:, j * tile : (j + 1) * tile] + jnp.where(meta[r, bands + first + j] > 0, 0.0, MASKED)
            for j in range(window)
        ]
        top, total, raised = softmax(parts)
        near = v_all[h][pl.ds(first, window)].reshape(window * tile, HEAD_DIM)
        near_sum[h][r] = jnp.dot(jnp.concatenate(raised, axis=1), near, preferred_element_type=jnp.float32)
        near_top[h][r] = jnp.broadcast_to(top, (tile, HEAD_DIM))
        near_total[h][r] = jnp.broadcast_to(total, (tile, HEAD_DIM))

    def attend_far(h, r):
        key_parts, value_parts, biases = [], [], []
        for side in range(2):
            for p in range(PICKS):
                at = 3 * bands + 2 * PICKS * (1 - side) + p
                index = meta[r, at]
                biases.append(jnp.where(meta[r, at + PICKS] > 0, 0.0, MASKED))
                key_parts.append(halo_in[side][h][0, index])
                value_parts.append(halo_in[side][h][1, index])
        far = jnp.concatenate(key_parts, axis=0)
        scores = lax.dot_general(q_all[h][r], far, across, preferred_element_type=jnp.float32)
        parts = [scores[:, j * tile : (j + 1) * tile] + bias for j, bias in enumerate(biases)]
        before = near_top[h][r][:, :1]
        top, total, raised = softmax(parts, before)
        kept = jnp.exp2((before - top) * scale)
        total = near_total[h][r][:, :1] * kept + total
        far = jnp.concatenate(value_parts, axis=0)
        result = jnp.dot(jnp.concatenate(raised, axis=1), far, preferred_element_type=jnp.float32)
        o_all[h][r] = ((near_sum[h][r] * kept + result) / total).astype(o_all[h].dtype)

    def give_back(h, peer):
        return pltpu.make_async_remote_copy(
            src_ref=o_all[h].at[peer],
            dst_ref=out.at[:, head_columns(me, h)],
            send_sem=o_send.at[h],
            recv_sem=o_recv.at[h],
            device_id={"space": peer},
            device_id_type=MESH,
        )

    def keep(h):
        return pltpu.make_async_copy(o_all[h].at[me], out.at[:, head_columns(me, h)], o_own.at[h])

    def near_loop(h):
        wait_spread(2, h)

        @pl.loop(0, bands, unroll=2)
        def _(r):
            attend_near(h, r)

    def far_loop(h):
        each_side(lambda copy: copy.wait_recv(), h, receive=True)

        @pl.loop(0, bands // 2)
        def _(i):
            places = [lax.rem(me + 2 * i + j + 1, bands) for j in range(2)]
            for r in places:
                attend_far(h, r)
            give_back(h, places[0]).start()

            @pl.when(i < bands // 2 - 1)
            def _():
                give_back(h, places[1]).start()

        keep(h).start()

    for h in range(heads):
        fill_halo(h)
        each_side(lambda copy: copy.start(), h)
    for h in range(heads):
        near_loop(h)
    for h in range(heads):
        far_loop(h)
    for h in range(heads):
        each_side(lambda copy: copy.wait_send(), h)

    for h in range(heads):
        for a in range(3):
            wait_bytes(moved[a][1][h], send_sem.at[a, h])
        for side in range(2):
            @pl.when(exists[side])
            def _():
                if h == 0:
                    ask(side).wait_send()
        wait_bytes(o_all[h], o_send.at[h])
        wait_bytes(o_all[h], o_recv.at[h])
        keep(h).wait()


def body(queries, keys, values, tile_mask):
    bands = lax.axis_size("space")
    groups = lax.axis_size("tm")
    tile, width = queries.shape
    heads = width // HEAD_DIM // bands
    whole = (bands, tile, HEAD_DIM)
    halo = (2, UMAX, tile, HEAD_DIM)
    dma = pltpu.SemaphoreType.DMA
    return pl.pallas_call(
        functools.partial(kernel, bands, groups, heads),
        out_shape=jax.ShapeDtypeStruct((tile, width), jnp.bfloat16),
        in_specs=[pl.BlockSpec(memory_space=pl.ANY)] * 4,
        out_specs=pl.BlockSpec(memory_space=pl.ANY),
        scratch_shapes=[pltpu.VMEM(whole, jnp.bfloat16)] * (4 * heads)
        + [pltpu.VMEM(halo, jnp.bfloat16)] * (4 * heads)
        + [pltpu.VMEM(whole, jnp.float32)] * (3 * heads)
        + [
            pltpu.VMEM(tile_mask.shape, jnp.int32),
            pltpu.VMEM((bands, LANES), jnp.int32),
            pltpu.SMEM((bands, LANES), jnp.int32),
            [pltpu.VMEM((8, LANES), jnp.int32)] * 2,
            [pltpu.VMEM((8, LANES), jnp.int32)] * 2,
            [pltpu.SMEM((8, LANES), jnp.int32)] * 2,
            dma,
            dma,
            dma((2,)),
            dma((2,)),
            dma((2,)),
            dma((3, heads)),
            dma((3, heads)),
            dma((3, heads)),
            dma((2, heads)),
            dma((2, heads)),
            dma((heads,)),
            dma((heads,)),
            dma((heads,)),
        ],
        compiler_params=pltpu.CompilerParams(
            collective_id=0, has_side_effects=True, vmem_limit_bytes=56 * 1024 * 1024
        ),
    )(tile_mask, queries, keys, values)


def solution(mesh):
    placed = (
        P(("tm", "space"), None),
        P(("tm", "space"), None),
        P(("tm", "space"), None),
        P("tm", None),
    )
    return jax.shard_map(
        body, mesh=mesh, in_specs=placed, out_specs=P(("tm", "space"), None), check_vma=False
    )
```

```python
import functools
import math

import jax
import jax.numpy as jnp
from jax import lax
from jax.experimental import pallas as pl
from jax.experimental.pallas import tpu as pltpu
from jax.sharding import PartitionSpec as P

HEAD_DIM = 128
REACH = 4
UMAX = 8
PICKS = 3
LANES = 128
MASKED = -1e30
MESH = pl.DeviceIdType.MESH


def plan(mask, g, bands):
    total = mask.shape[1]
    near = pltpu.roll(mask, lax.rem(2 * total - (g - 1) * bands, total), 1)[:, :LANES]
    lane = lax.broadcasted_iota(jnp.int32, near.shape, 1)
    list_lane = lax.broadcasted_iota(jnp.int32, (8, LANES), 1)
    used = jnp.max(near, axis=0, keepdims=True)
    packed = jnp.where(lane < 3 * bands, near, 0)
    lists = []
    for side, base in enumerate((2 * bands, 0)):
        place = jnp.zeros((1, LANES), jnp.int32)
        order = jnp.zeros_like(near)
        picks = [jnp.zeros_like(near) for _ in range(PICKS)]
        tiles = jnp.zeros((8, LANES), jnp.int32)
        for c in range(bands):
            taken = jnp.broadcast_to(near[:, base + c : base + c + 1], near.shape)
            wanted = jnp.broadcast_to(used[:, base + c : base + c + 1], (1, LANES))
            tiles = tiles + jnp.where((wanted > 0) & (list_lane == place), c, 0)
            for p in range(PICKS):
                picks[p] = picks[p] + jnp.where((taken > 0) & (order == p), place, 0)
            place = place + wanted
            order = order + taken
        at = 3 * bands + 2 * PICKS * side
        for p in range(PICKS):
            packed = jnp.where(lane == at + p, picks[p], packed)
            packed = jnp.where(lane == at + PICKS + p, jnp.where(order > p, 1, 0), packed)
        lists.append(tiles)
    return packed, lists


def kernel(bands, groups, heads, mask_in, q_in, k_in, v_in, out, *scratch):
    q_all, k_all, v_all, o_all = (scratch[i * heads : (i + 1) * heads] for i in range(4))
    halo_out = [scratch[(4 + i) * heads : (5 + i) * heads] for i in range(2)]
    halo_in = [scratch[(6 + i) * heads : (7 + i) * heads] for i in range(2)]
    near_sum, near_top, near_total = (scratch[(8 + i) * heads : (9 + i) * heads] for i in range(3))
    (
        mask, packed, meta, wants, asked, lists,
        mask_sem, meta_sem, ask_send, ask_recv, ask_own,
        own_sem, send_sem, recv_sem, halo_send, halo_recv, o_own, o_send, o_recv,
    ) = scratch[11 * heads :]
    g = lax.axis_index("tm")
    me = lax.axis_index("space")
    tile = q_in.shape[0]
    window = min(2 * REACH + 1, bands)
    exists = (g < groups - 1, g > 0)
    moved = ((k_in, k_all), (v_in, v_all), (q_in, q_all))

    barrier = pltpu.get_barrier_semaphore()
    fetch_mask = pltpu.make_async_copy(mask_in, mask, mask_sem)
    fetch_mask.start()

    @pl.loop(1, bands)
    def _(d):
        pl.semaphore_signal(barrier, inc=1, device_id={"space": lax.rem(me + d, bands)}, device_id_type=MESH)

    for step in (1, groups - 1):
        pl.semaphore_signal(barrier, inc=1, device_id={"tm": lax.rem(g + step, groups)}, device_id_type=MESH)

    def place(i):
        half, low = lax.rem(me // 2, 2), lax.rem(me, 2)
        other = jnp.where(i < bands // 2, 1 - half, half)
        x = lax.rem(me // 4 + lax.rem(i, bands // 2) // 2, bands // 4)
        return x * 4 + other * 2 + lax.rem(low + i, 2)

    def head_columns(owner, h):
        return pl.ds(pl.multiple_of((owner * heads + h) * HEAD_DIM, HEAD_DIM), HEAD_DIM)

    def own_copy(a, h):
        source, target = moved[a]
        return pltpu.make_async_copy(source.at[:, head_columns(me, h)], target[h].at[me], own_sem.at[a, h])

    pl.semaphore_wait(barrier, bands + 1)

    def ask(side):
        return pltpu.make_async_remote_copy(
            src_ref=wants[side],
            dst_ref=asked[1 - side],
            send_sem=ask_send.at[side],
            recv_sem=ask_recv.at[1 - side],
            device_id={"tm": g + 1 if side == 0 else g - 1},
            device_id_type=MESH,
        )

    def spread(a, h, peer):
        source, target = moved[a]
        return pltpu.make_async_remote_copy(
            src_ref=source.at[:, head_columns(peer, h)],
            dst_ref=target[h].at[me],
            send_sem=send_sem.at[a, h],
            recv_sem=recv_sem.at[a, h],
            device_id={"space": peer},
            device_id_type=MESH,
        )

    def start_spread(a, h):
        @pl.loop(0, bands // 2)
        def _(i):
            spread(a, h, place(i)).start()

        @pl.loop(bands // 2 + 1, bands)
        def _(i):
            spread(a, h, place(i)).start()

    def wait_bytes(buffer, sem):
        part = buffer.at[pl.ds(0, bands - 1)]
        pltpu.make_async_copy(part, part, sem).wait()

    def wait_spread(a, h):
        wait_bytes(moved[a][1][h], recv_sem.at[a, h])
        own_copy(a, h).wait()

    def sent(a, h):
        wait_bytes(moved[a][1][h], send_sem.at[a, h])

    start_spread(0, 0)
    start_spread(1, 0)
    start_spread(0, 1)
    start_spread(1, 1)
    for h in range(heads):
        for a in range(3):
            own_copy(a, h).start()

    fetch_mask.wait()
    packed[...], found = plan(mask[...], g, bands)
    for side in range(2):
        wants[side][...] = found[side]
    fetch_meta = pltpu.make_async_copy(packed, meta, meta_sem)
    fetch_meta.start()

    for side in range(2):
        @pl.when(exists[side])
        def _():
            ask(side).start()

    def halo(side, h, s=None):
        return pltpu.make_async_remote_copy(
            src_ref=halo_out[side][h] if s is None else halo_out[side][h].at[:, s],
            dst_ref=halo_in[side][h] if s is None else halo_in[side][h].at[:, s],
            send_sem=halo_send.at[side, h],
            recv_sem=halo_recv.at[side, h],
            device_id={"tm": g + 1 if side == 0 else g - 1},
            device_id_type=MESH,
        )

    def fetch_list(side):
        return pltpu.make_async_copy(asked[side], lists[side], ask_own.at[side])

    for side in range(2):
        @pl.when(jnp.logical_not(exists[1 - side]))
        def _():
            for h in range(heads):
                halo_in[side][h][...] = jnp.zeros(halo_in[side][h].shape, halo_in[side][h].dtype)

    fetch_meta.wait()
    for side in range(2):
        @pl.when(exists[side])
        def _():
            ask(1 - side).wait_recv()
            fetch_list(side).start()

    for side in range(2):
        @pl.when(exists[side])
        def _():
            fetch_list(side).wait()

    def fill_halo(h, at_once=True):
        wait_spread(0, h)
        wait_spread(1, h)
        for side in range(2):
            @pl.when(exists[side])
            def _():
                for s in range(UMAX):
                    index = lists[side][0, s]
                    halo_out[side][h][0, s] = k_all[h][index]
                    halo_out[side][h][1, s] = v_all[h][index]
                    if at_once:
                        halo(side, h, s).start()

    def start_halo(h):
        for side in range(2):
            @pl.when(exists[side])
            def _():
                for s in range(UMAX):
                    halo(side, h, s).start()

    def each_side(action, h, receive=False):
        for side in range(2):
            @pl.when(exists[1 - side if receive else side])
            def _():
                action(halo(side, h))

    scale = math.log2(math.e) / math.sqrt(HEAD_DIM)
    across = (((1,), (1,)), ((), ()))

    def softmax(parts, floor=None):
        top = jnp.max(functools.reduce(jnp.maximum, parts), axis=1, keepdims=True)
        if floor is not None:
            top = jnp.maximum(top, floor)
        raised = [jnp.exp2((part - top) * scale) for part in parts]
        total = jnp.sum(functools.reduce(jnp.add, raised), axis=1, keepdims=True)
        return top, total, [one.astype(jnp.bfloat16) for one in raised]

    def attend_near(h, r):
        first = jnp.clip(r - REACH, 0, bands - window)
        near = k_all[h][pl.ds(first, window)].reshape(window * tile, HEAD_DIM)
        scores = lax.dot_general(q_all[h][r], near, across, preferred_element_type=jnp.float32)
        parts = [
            scores[:, j * tile : (j + 1) * tile] + jnp.where(meta[r, bands + first + j] > 0, 0.0, MASKED)
            for j in range(window)
        ]
        top, total, raised = softmax(parts)
        near = v_all[h][pl.ds(first, window)].reshape(window * tile, HEAD_DIM)
        near_sum[h][r] = jnp.dot(jnp.concatenate(raised, axis=1), near, preferred_element_type=jnp.float32)
        near_top[h][r] = jnp.broadcast_to(top, (tile, HEAD_DIM))
        near_total[h][r] = jnp.broadcast_to(total, (tile, HEAD_DIM))

    def attend_far(h, r):
        key_parts, value_parts, biases = [], [], []
        for side in range(2):
            for p in range(PICKS):
                at = 3 * bands + 2 * PICKS * (1 - side) + p
                index = meta[r, at]
                biases.append(jnp.where(meta[r, at + PICKS] > 0, 0.0, MASKED))
                key_parts.append(halo_in[side][h][0, index])
                value_parts.append(halo_in[side][h][1, index])
        far = jnp.concatenate(key_parts, axis=0)
        scores = lax.dot_general(q_all[h][r], far, across, preferred_element_type=jnp.float32)
        parts = [scores[:, j * tile : (j + 1) * tile] + bias for j, bias in enumerate(biases)]
        before = near_top[h][r][:, :1]
        top, total, raised = softmax(parts, before)
        kept = jnp.exp2((before - top) * scale)
        total = near_total[h][r][:, :1] * kept + total
        far = jnp.concatenate(value_parts, axis=0)
        result = jnp.dot(jnp.concatenate(raised, axis=1), far, preferred_element_type=jnp.float32)
        o_all[h][r] = ((near_sum[h][r] * kept + result) / total).astype(o_all[h].dtype)

    def give_back(h, peer):
        return pltpu.make_async_remote_copy(
            src_ref=o_all[h].at[peer],
            dst_ref=out.at[:, head_columns(me, h)],
            send_sem=o_send.at[h],
            recv_sem=o_recv.at[h],
            device_id={"space": peer},
            device_id_type=MESH,
        )

    def keep(h):
        return pltpu.make_async_copy(o_all[h].at[me], out.at[:, head_columns(me, h)], o_own.at[h])

    def near_loop(h):
        wait_spread(2, h)

        @pl.loop(0, bands, unroll=2)
        def _(r):
            attend_near(h, r)

    def far_loop(h):
        each_side(lambda copy: copy.wait_recv(), h, receive=True)

        @pl.loop(0, bands // 2)
        def _(i):
            places = [place(2 * i + j) for j in range(2)]
            for r in places:
                attend_far(h, r)

            @pl.when(i != bands // 4)
            def _():
                give_back(h, places[0]).start()

            give_back(h, places[1]).start()

        keep(h).start()

    sent(0, 0)
    sent(1, 0)
    sent(0, 1)
    sent(1, 1)
    start_spread(2, 0)
    start_spread(2, 1)
    fill_halo(0)
    fill_halo(1)
    near_loop(0)
    near_loop(1)
    far_loop(0)
    far_loop(1)
    each_side(lambda copy: copy.wait_send(), 0)
    each_side(lambda copy: copy.wait_send(), 1)
    sent(2, 0)
    sent(2, 1)

    for h in range(heads):
        for side in range(2):
            @pl.when(exists[side])
            def _():
                if h == 0:
                    ask(side).wait_send()
        wait_bytes(o_all[h], o_send.at[h])
        wait_bytes(o_all[h], o_recv.at[h])
        keep(h).wait()


def body(queries, keys, values, tile_mask):
    bands = lax.axis_size("space")
    groups = lax.axis_size("tm")
    tile, width = queries.shape
    heads = width // HEAD_DIM // bands
    whole = (bands, tile, HEAD_DIM)
    halo = (2, UMAX, tile, HEAD_DIM)
    dma = pltpu.SemaphoreType.DMA
    return pl.pallas_call(
        functools.partial(kernel, bands, groups, heads),
        out_shape=pltpu.VMEM((tile, width), jnp.bfloat16),
        in_specs=[pl.BlockSpec(memory_space=pltpu.HBM)] * 4,
        out_specs=pl.BlockSpec(memory_space=pl.ANY),
        scratch_shapes=[pltpu.VMEM(whole, jnp.bfloat16)] * (4 * heads)
        + [pltpu.VMEM(halo, jnp.bfloat16)] * (4 * heads)
        + [pltpu.VMEM(whole, jnp.float32)] * (3 * heads)
        + [
            pltpu.VMEM(tile_mask.shape, jnp.int32),
            pltpu.VMEM((bands, LANES), jnp.int32),
            pltpu.SMEM((bands, LANES), jnp.int32),
            [pltpu.VMEM((8, LANES), jnp.int32)] * 2,
            [pltpu.VMEM((8, LANES), jnp.int32)] * 2,
            [pltpu.SMEM((8, LANES), jnp.int32)] * 2,
            dma,
            dma,
            dma((2,)),
            dma((2,)),
            dma((2,)),
            dma((3, heads)),
            dma((3, heads)),
            dma((3, heads)),
            dma((2, heads)),
            dma((2, heads)),
            dma((heads,)),
            dma((heads,)),
            dma((heads,)),
        ],
        compiler_params=pltpu.CompilerParams(
            collective_id=0, has_side_effects=True, vmem_limit_bytes=56 * 1024 * 1024
        ),
    )(tile_mask, queries, keys, values)


def solution(mesh):
    placed = (
        P(("tm", "space"), None),
        P(("tm", "space"), None),
        P(("tm", "space"), None),
        P("tm", None),
    )
    return jax.shard_map(
        body, mesh=mesh, in_specs=placed, out_specs=P(("tm", "space"), None), check_vma=False
    )
```

```python
import functools
import math

import jax
import jax.numpy as jnp
from jax import lax
from jax.experimental import pallas as pl
from jax.experimental.pallas import tpu as pltpu
from jax.sharding import PartitionSpec as P

HEAD_DIM = 128
REACH = 4
UMAX = 8
PICKS = 3
LANES = 128
MASKED = -1e30
RUN = 8
MESH = pl.DeviceIdType.MESH


def plan(mask, g, bands):
    total = mask.shape[1]
    near = pltpu.roll(mask, lax.rem(2 * total - (g - 1) * bands, total), 1)[:, :LANES]
    lane = lax.broadcasted_iota(jnp.int32, near.shape, 1)
    list_lane = lax.broadcasted_iota(jnp.int32, (8, LANES), 1)
    used = jnp.max(near, axis=0, keepdims=True)
    packed = jnp.where(lane < 3 * bands, near, 0)
    lists = []
    for side, base in enumerate((2 * bands, 0)):
        place = jnp.zeros((1, LANES), jnp.int32)
        order = jnp.zeros_like(near)
        picks = [jnp.zeros_like(near) for _ in range(PICKS)]
        tiles = jnp.zeros((8, LANES), jnp.int32)
        for c in range(bands):
            taken = jnp.broadcast_to(near[:, base + c : base + c + 1], near.shape)
            wanted = jnp.broadcast_to(used[:, base + c : base + c + 1], (1, LANES))
            tiles = tiles + jnp.where((wanted > 0) & (list_lane == place), c, 0)
            for p in range(PICKS):
                picks[p] = picks[p] + jnp.where((taken > 0) & (order == p), place, 0)
            place = place + wanted
            order = order + taken
        at = 3 * bands + 2 * PICKS * side
        for p in range(PICKS):
            packed = jnp.where(lane == at + p, picks[p], packed)
            packed = jnp.where(lane == at + PICKS + p, jnp.where(order > p, 1, 0), packed)
        lists.append(tiles)
    return packed, lists


def kernel(bands, groups, heads, mask_in, q_in, k_in, v_in, out, *scratch):
    q_all, k_all, v_all, o_all = (scratch[i * heads : (i + 1) * heads] for i in range(4))
    halo_out = [scratch[(4 + i) * heads : (5 + i) * heads] for i in range(2)]
    halo_in = [scratch[(6 + i) * heads : (7 + i) * heads] for i in range(2)]
    near_sum, near_top, near_total = (scratch[(8 + i) * heads : (9 + i) * heads] for i in range(3))
    (
        mask, packed, meta, wants, asked, lists,
        mask_sem, meta_sem, ask_send, ask_recv, ask_own,
        own_sem, send_sem, recv_sem, halo_send, halo_recv, o_own, o_send, o_recv,
    ) = scratch[11 * heads :]
    g = lax.axis_index("tm")
    me = lax.axis_index("space")
    tile = q_in.shape[0]
    window = min(2 * REACH + 1, bands)
    even = lax.rem(g, 2) == 0
    beside = (jnp.where(even, g + 1, g - 1), jnp.where(even, g - 1, g + 1))
    exists = (g >= 0, (beside[1] >= 0) & (beside[1] < groups))
    moved = ((k_in, k_all), (v_in, v_all), (q_in, q_all))

    barrier = pltpu.get_barrier_semaphore()
    fetch_mask = pltpu.make_async_copy(mask_in, mask, mask_sem)
    fetch_mask.start()

    @pl.loop(1, bands)
    def _(d):
        pl.semaphore_signal(barrier, inc=1, device_id={"space": lax.rem(me + d, bands)}, device_id_type=MESH)

    def place(i):
        half, low = lax.rem(me // 2, 2), lax.rem(me, 2)
        other = jnp.where(i < bands // 2, 1 - half, half)
        x = lax.rem(me // 4 + lax.rem(i, bands // 2) // 2, bands // 4)
        return x * 4 + other * 2 + lax.rem(low + i, 2)

    def head_columns(owner, h):
        return pl.ds(pl.multiple_of((owner * heads + h) * HEAD_DIM, HEAD_DIM), HEAD_DIM)

    def own_copy(a, h):
        source, target = moved[a]
        return pltpu.make_async_copy(source.at[:, head_columns(me, h)], target[h].at[me], own_sem.at[a, h])

    late_left = (g > 0) & even & (lax.rem(g, RUN) != 0)
    late_right = (g < groups - 1) & (even | (lax.rem(g, RUN) == RUN - 1))
    at_entry = late_left.astype(jnp.int32) + late_right.astype(jnp.int32)
    pl.semaphore_wait(barrier, bands - 1 + at_entry)

    for side in range(2):
        @pl.when(exists[side])
        def _():
            pl.semaphore_signal(barrier, inc=1, device_id={"tm": beside[side]}, device_id_type=MESH)

    def ask(side):
        return pltpu.make_async_remote_copy(
            src_ref=wants[side],
            dst_ref=asked[side],
            send_sem=ask_send.at[side],
            recv_sem=ask_recv.at[side],
            device_id={"tm": beside[side]},
            device_id_type=MESH,
        )

    def spread(a, h, peer):
        source, target = moved[a]
        return pltpu.make_async_remote_copy(
            src_ref=source.at[:, head_columns(peer, h)],
            dst_ref=target[h].at[me],
            send_sem=send_sem.at[a, h],
            recv_sem=recv_sem.at[a, h],
            device_id={"space": peer},
            device_id_type=MESH,
        )

    def start_spread(a, h):
        @pl.loop(0, bands // 2)
        def _(i):
            spread(a, h, place(i)).start()

        @pl.loop(bands // 2 + 1, bands)
        def _(i):
            spread(a, h, place(i)).start()

    def wait_bytes(buffer, sem):
        part = buffer.at[pl.ds(0, bands - 1)]
        pltpu.make_async_copy(part, part, sem).wait()

    def wait_spread(a, h):
        wait_bytes(moved[a][1][h], recv_sem.at[a, h])
        own_copy(a, h).wait()

    def sent(a, h):
        wait_bytes(moved[a][1][h], send_sem.at[a, h])

    start_spread(0, 0)
    start_spread(1, 0)
    start_spread(0, 1)
    start_spread(1, 1)
    for h in range(heads):
        for a in range(3):
            own_copy(a, h).start()

    fetch_mask.wait()
    packed[...], found = plan(mask[...], g, bands)
    for side in range(2):
        wants[side][...] = jnp.where(even, found[side], found[1 - side])
    fetch_meta = pltpu.make_async_copy(packed, meta, meta_sem)
    fetch_meta.start()

    to_come = 1 + exists[1].astype(jnp.int32) - at_entry

    @pl.when(to_come > 0)
    def _():
        pl.semaphore_wait(barrier, to_come)

    for side in range(2):
        @pl.when(exists[side])
        def _():
            ask(side).start()

    def halo(side, h, s=None):
        return pltpu.make_async_remote_copy(
            src_ref=halo_out[side][h] if s is None else halo_out[side][h].at[:, s],
            dst_ref=halo_in[side][h] if s is None else halo_in[side][h].at[:, s],
            send_sem=halo_send.at[side, h],
            recv_sem=halo_recv.at[side, h],
            device_id={"tm": beside[side]},
            device_id_type=MESH,
        )

    def fetch_list(side):
        return pltpu.make_async_copy(asked[side], lists[side], ask_own.at[side])

    @pl.when(jnp.logical_not(exists[1]))
    def _():
        for h in range(heads):
            halo_in[1][h][...] = jnp.zeros(halo_in[1][h].shape, halo_in[1][h].dtype)

    fetch_meta.wait()
    for side in range(2):
        @pl.when(exists[side])
        def _():
            ask(side).wait_recv()
            fetch_list(side).start()

    for side in range(2):
        @pl.when(exists[side])
        def _():
            fetch_list(side).wait()

    def fill_halo(h):
        wait_spread(0, h)
        wait_spread(1, h)
        for side in (1, 0):
            @pl.when(exists[side])
            def _():
                for s in range(UMAX):
                    index = lists[side][0, s]
                    halo_out[side][h][0, s] = k_all[h][index]
                    halo_out[side][h][1, s] = v_all[h][index]
                    halo(side, h, s).start()

    scale = math.log2(math.e) / math.sqrt(HEAD_DIM)
    across = (((1,), (1,)), ((), ()))

    def softmax(parts, floor=None):
        top = jnp.max(functools.reduce(jnp.maximum, parts), axis=1, keepdims=True)
        if floor is not None:
            top = jnp.maximum(top, floor)
        raised = [jnp.exp2((part - top) * scale) for part in parts]
        total = jnp.sum(functools.reduce(jnp.add, raised), axis=1, keepdims=True)
        return top, total, [one.astype(jnp.bfloat16) for one in raised]

    def picked(side, h, r):
        key_parts, value_parts, biases = [], [], []
        for p in range(PICKS):
            at = 3 * bands + PICKS * 2 * jnp.where(even, side, 1 - side) + p
            index = meta[r, at]
            biases.append(jnp.where(meta[r, at + PICKS] > 0, 0.0, MASKED))
            key_parts.append(halo_in[side][h][0, index])
            value_parts.append(halo_in[side][h][1, index])
        far = jnp.concatenate(key_parts, axis=0)
        scores = lax.dot_general(q_all[h][r], far, across, preferred_element_type=jnp.float32)
        parts = [scores[:, j * tile : (j + 1) * tile] + bias for j, bias in enumerate(biases)]
        return parts, jnp.concatenate(value_parts, axis=0)

    def attend_near(h, r):
        first = jnp.clip(r - REACH, 0, bands - window)
        near = k_all[h][pl.ds(first, window)].reshape(window * tile, HEAD_DIM)
        scores = lax.dot_general(q_all[h][r], near, across, preferred_element_type=jnp.float32)
        parts = [
            scores[:, j * tile : (j + 1) * tile] + jnp.where(meta[r, bands + first + j] > 0, 0.0, MASKED)
            for j in range(window)
        ]
        more, far = picked(0, h, r)
        top, total, raised = softmax(parts + more)
        near = v_all[h][pl.ds(first, window)].reshape(window * tile, HEAD_DIM)
        near_sum[h][r] = jnp.dot(
            jnp.concatenate(raised[:window], axis=1), near, preferred_element_type=jnp.float32
        ) + jnp.dot(jnp.concatenate(raised[window:], axis=1), far, preferred_element_type=jnp.float32)
        near_top[h][r] = jnp.broadcast_to(top, (tile, HEAD_DIM))
        near_total[h][r] = jnp.broadcast_to(total, (tile, HEAD_DIM))

    def attend_far(h, r):
        parts, far = picked(1, h, r)
        before = near_top[h][r][:, :1]
        top, total, raised = softmax(parts, before)
        kept = jnp.exp2((before - top) * scale)
        total = near_total[h][r][:, :1] * kept + total
        result = jnp.dot(jnp.concatenate(raised, axis=1), far, preferred_element_type=jnp.float32)
        o_all[h][r] = ((near_sum[h][r] * kept + result) / total).astype(o_all[h].dtype)

    def give_back(h, peer):
        return pltpu.make_async_remote_copy(
            src_ref=o_all[h].at[peer],
            dst_ref=out.at[:, head_columns(me, h)],
            send_sem=o_send.at[h],
            recv_sem=o_recv.at[h],
            device_id={"space": peer},
            device_id_type=MESH,
        )

    def keep(h):
        return pltpu.make_async_copy(o_all[h].at[me], out.at[:, head_columns(me, h)], o_own.at[h])

    def near_loop(h):
        wait_spread(2, h)
        halo(0, h).wait_recv()

        @pl.loop(0, bands, unroll=2)
        def _(r):
            attend_near(h, r)

    def far_loop(h):
        @pl.when(exists[1])
        def _():
            halo(1, h).wait_recv()

        @pl.loop(0, bands // 2)
        def _(i):
            places = [place(2 * i + j) for j in range(2)]
            for r in places:
                attend_far(h, r)

            @pl.when(i != bands // 4)
            def _():
                give_back(h, places[0]).start()

            give_back(h, places[1]).start()

        keep(h).start()

    sent(0, 0)
    sent(1, 0)
    sent(0, 1)
    sent(1, 1)
    start_spread(2, 0)
    fill_halo(0)
    start_spread(2, 1)
    fill_halo(1)
    near_loop(0)
    near_loop(1)
    far_loop(0)
    far_loop(1)
    sent(2, 0)
    sent(2, 1)

    for h in range(heads):
        for side in range(2):
            @pl.when(exists[side])
            def _():
                halo(side, h).wait_send()
                if h == 0:
                    ask(side).wait_send()
        wait_bytes(o_all[h], o_send.at[h])
        wait_bytes(o_all[h], o_recv.at[h])
        keep(h).wait()


def body(queries, keys, values, tile_mask):
    bands = lax.axis_size("space")
    groups = lax.axis_size("tm")
    tile, width = queries.shape
    heads = width // HEAD_DIM // bands
    whole = (bands, tile, HEAD_DIM)
    halo = (2, UMAX, tile, HEAD_DIM)
    dma = pltpu.SemaphoreType.DMA
    return pl.pallas_call(
        functools.partial(kernel, bands, groups, heads),
        out_shape=pltpu.VMEM((tile, width), jnp.bfloat16),
        in_specs=[pl.BlockSpec(memory_space=pltpu.HBM)] * 4,
        out_specs=pl.BlockSpec(memory_space=pl.ANY),
        scratch_shapes=[pltpu.VMEM(whole, jnp.bfloat16)] * (4 * heads)
        + [pltpu.VMEM(halo, jnp.bfloat16)] * (4 * heads)
        + [pltpu.VMEM(whole, jnp.float32)] * (3 * heads)
        + [
            pltpu.VMEM(tile_mask.shape, jnp.int32),
            pltpu.VMEM((bands, LANES), jnp.int32),
            pltpu.SMEM((bands, LANES), jnp.int32),
            [pltpu.VMEM((8, LANES), jnp.int32)] * 2,
            [pltpu.VMEM((8, LANES), jnp.int32)] * 2,
            [pltpu.SMEM((8, LANES), jnp.int32)] * 2,
            dma,
            dma,
            dma((2,)),
            dma((2,)),
            dma((2,)),
            dma((3, heads)),
            dma((3, heads)),
            dma((3, heads)),
            dma((2, heads)),
            dma((2, heads)),
            dma((heads,)),
            dma((heads,)),
            dma((heads,)),
        ],
        compiler_params=pltpu.CompilerParams(
            collective_id=0, has_side_effects=True, vmem_limit_bytes=56 * 1024 * 1024
        ),
    )(tile_mask, queries, keys, values)


def solution(mesh):
    placed = (
        P(("tm", "space"), None),
        P(("tm", "space"), None),
        P(("tm", "space"), None),
        P("tm", None),
    )
    return jax.shard_map(
        body, mesh=mesh, in_specs=placed, out_specs=P(("tm", "space"), None), check_vma=False
    )
```

```python
import functools
import math

import jax
import jax.numpy as jnp
from jax import lax
from jax.experimental import pallas as pl
from jax.experimental.pallas import tpu as pltpu
from jax.sharding import PartitionSpec as P

HEAD_DIM = 128
REACH = 4
UMAX = 8
PICKS = 3
LANES = 128
MASKED = -1e30
RUN = 8
MESH = pl.DeviceIdType.MESH


def plan(mask, g, bands):
    total = mask.shape[1]
    near = pltpu.roll(mask, lax.rem(2 * total - (g - 1) * bands, total), 1)[:, :LANES]
    lane = lax.broadcasted_iota(jnp.int32, near.shape, 1)
    list_lane = lax.broadcasted_iota(jnp.int32, (8, LANES), 1)
    used = jnp.max(near, axis=0, keepdims=True)
    packed = jnp.where(lane < 3 * bands, near, 0)
    lists = []
    for side, base in enumerate((2 * bands, 0)):
        place = jnp.zeros((1, LANES), jnp.int32)
        order = jnp.zeros_like(near)
        picks = [jnp.zeros_like(near) for _ in range(PICKS)]
        tiles = jnp.zeros((8, LANES), jnp.int32)
        for c in range(bands):
            taken = jnp.broadcast_to(near[:, base + c : base + c + 1], near.shape)
            wanted = jnp.broadcast_to(used[:, base + c : base + c + 1], (1, LANES))
            tiles = tiles + jnp.where((wanted > 0) & (list_lane == place), c, 0)
            for p in range(PICKS):
                picks[p] = picks[p] + jnp.where((taken > 0) & (order == p), place, 0)
            place = place + wanted
            order = order + taken
        at = 3 * bands + 2 * PICKS * side
        for p in range(PICKS):
            packed = jnp.where(lane == at + p, picks[p], packed)
            packed = jnp.where(lane == at + PICKS + p, jnp.where(order > p, 1, 0), packed)
        lists.append(tiles)
    return packed, lists


def kernel(bands, groups, heads, mask_in, q_in, k_in, v_in, out, *scratch):
    q_all, k_all, v_all, o_all = (scratch[i * heads : (i + 1) * heads] for i in range(4))
    halo_out = [scratch[(4 + i) * heads : (5 + i) * heads] for i in range(2)]
    halo_in = [scratch[(6 + i) * heads : (7 + i) * heads] for i in range(2)]
    near_sum, near_top, near_total = (scratch[(8 + i) * heads : (9 + i) * heads] for i in range(3))
    (
        mask, packed, meta, wants, asked, lists,
        mask_sem, meta_sem, ask_send, ask_recv, ask_own,
        own_sem, send_sem, recv_sem, halo_send, halo_recv, o_own, o_send, o_recv,
    ) = scratch[11 * heads :]
    g = lax.axis_index("tm")
    me = lax.axis_index("space")
    tile = q_in.shape[0]
    window = min(2 * REACH + 1, bands)
    even = lax.rem(g, 2) == 0
    beside = (jnp.where(even, g + 1, g - 1), jnp.where(even, g - 1, g + 1))
    exists = (g >= 0, (beside[1] >= 0) & (beside[1] < groups))
    moved = ((k_in, k_all), (v_in, v_all), (q_in, q_all))

    barrier = pltpu.get_barrier_semaphore()
    fetch_mask = pltpu.make_async_copy(mask_in, mask, mask_sem)
    fetch_mask.start()

    @pl.loop(1, bands)
    def _(d):
        pl.semaphore_signal(barrier, inc=1, device_id={"space": lax.rem(me + d, bands)}, device_id_type=MESH)

    def place(i):
        half, low = lax.rem(me // 2, 2), lax.rem(me, 2)
        other = jnp.where(i < bands // 2, 1 - half, half)
        x = lax.rem(me // 4 + lax.rem(i, bands // 2) // 2, bands // 4)
        return x * 4 + other * 2 + lax.rem(low + i, 2)

    def head_columns(owner, h):
        return pl.ds(pl.multiple_of((owner * heads + h) * HEAD_DIM, HEAD_DIM), HEAD_DIM)

    def own_copy(a, h):
        source, target = moved[a]
        return pltpu.make_async_copy(source.at[:, head_columns(me, h)], target[h].at[me], own_sem.at[a, h])

    late_left = (g > 0) & even & (lax.rem(g, RUN) != 0)
    late_right = (g < groups - 1) & (even | (lax.rem(g, RUN) == RUN - 1))
    at_entry = late_left.astype(jnp.int32) + late_right.astype(jnp.int32)
    pl.semaphore_wait(barrier, bands - 1 + at_entry)

    for side in range(2):
        @pl.when(exists[side])
        def _():
            pl.semaphore_signal(barrier, inc=1, device_id={"tm": beside[side]}, device_id_type=MESH)

    def ask(side):
        return pltpu.make_async_remote_copy(
            src_ref=wants[side],
            dst_ref=asked[side],
            send_sem=ask_send.at[side],
            recv_sem=ask_recv.at[side],
            device_id={"tm": beside[side]},
            device_id_type=MESH,
        )

    def spread(a, h, peer):
        source, target = moved[a]
        return pltpu.make_async_remote_copy(
            src_ref=source.at[:, head_columns(peer, h)],
            dst_ref=target[h].at[me],
            send_sem=send_sem.at[a, h],
            recv_sem=recv_sem.at[a, h],
            device_id={"space": peer},
            device_id_type=MESH,
        )

    def start_spread(arrays, h):
        @pl.loop(0, bands // 2)
        def _(i):
            for a in arrays:
                spread(a, h, place(i)).start()

        @pl.loop(bands // 2 + 1, bands)
        def _(i):
            for a in arrays:
                spread(a, h, place(i)).start()

    def wait_bytes(buffer, sem):
        part = buffer.at[pl.ds(0, bands - 1)]
        pltpu.make_async_copy(part, part, sem).wait()

    def wait_spread(a, h):
        wait_bytes(moved[a][1][h], recv_sem.at[a, h])
        own_copy(a, h).wait()

    def sent(a, h):
        wait_bytes(moved[a][1][h], send_sem.at[a, h])

    for h in range(heads):
        start_spread((0, 1), h)
    for h in range(heads):
        for a in range(3):
            own_copy(a, h).start()

    fetch_mask.wait()
    packed[...], found = plan(mask[...], g, bands)
    for side in range(2):
        wants[side][...] = jnp.where(even, found[side], found[1 - side])
    fetch_meta = pltpu.make_async_copy(packed, meta, meta_sem)
    fetch_meta.start()

    to_come = 1 + exists[1].astype(jnp.int32) - at_entry

    @pl.when(to_come > 0)
    def _():
        pl.semaphore_wait(barrier, to_come)

    for side in range(2):
        @pl.when(exists[side])
        def _():
            ask(side).start()

    def halo(side, h, s=None):
        return pltpu.make_async_remote_copy(
            src_ref=halo_out[side][h] if s is None else halo_out[side][h].at[:, s],
            dst_ref=halo_in[side][h] if s is None else halo_in[side][h].at[:, s],
            send_sem=halo_send.at[side, h],
            recv_sem=halo_recv.at[side, h],
            device_id={"tm": beside[side]},
            device_id_type=MESH,
        )

    def fetch_list(side):
        return pltpu.make_async_copy(asked[side], lists[side], ask_own.at[side])

    @pl.when(jnp.logical_not(exists[1]))
    def _():
        for h in range(heads):
            halo_in[1][h][...] = jnp.zeros(halo_in[1][h].shape, halo_in[1][h].dtype)

    fetch_meta.wait()
    for side in range(2):
        @pl.when(exists[side])
        def _():
            ask(side).wait_recv()
            fetch_list(side).start()

    for side in range(2):
        @pl.when(exists[side])
        def _():
            fetch_list(side).wait()

    def fill_halo(h):
        wait_spread(0, h)
        wait_spread(1, h)
        for side in (1, 0):
            @pl.when(exists[side])
            def _():
                for s in range(UMAX):
                    index = lists[side][0, s]
                    halo_out[side][h][0, s] = k_all[h][index]
                    halo_out[side][h][1, s] = v_all[h][index]
                    halo(side, h, s).start()

    scale = math.log2(math.e) / math.sqrt(HEAD_DIM)
    across = (((1,), (1,)), ((), ()))

    def softmax(parts, floor=None):
        top = jnp.max(functools.reduce(jnp.maximum, parts), axis=1, keepdims=True)
        if floor is not None:
            top = jnp.maximum(top, floor)
        raised = [jnp.exp2((part - top) * scale) for part in parts]
        total = jnp.sum(functools.reduce(jnp.add, raised), axis=1, keepdims=True)
        return top, total, [one.astype(jnp.bfloat16) for one in raised]

    def picked(side, h, r):
        key_parts, value_parts, biases = [], [], []
        for p in range(PICKS):
            at = 3 * bands + PICKS * 2 * jnp.where(even, side, 1 - side) + p
            index = meta[r, at]
            biases.append(jnp.where(meta[r, at + PICKS] > 0, 0.0, MASKED))
            key_parts.append(halo_in[side][h][0, index])
            value_parts.append(halo_in[side][h][1, index])
        far = jnp.concatenate(key_parts, axis=0)
        scores = lax.dot_general(q_all[h][r], far, across, preferred_element_type=jnp.float32)
        parts = [scores[:, j * tile : (j + 1) * tile] + bias for j, bias in enumerate(biases)]
        return parts, jnp.concatenate(value_parts, axis=0)

    def attend_near(h, r):
        first = jnp.clip(r - REACH, 0, bands - window)
        near = k_all[h][pl.ds(first, window)].reshape(window * tile, HEAD_DIM)
        scores = lax.dot_general(q_all[h][r], near, across, preferred_element_type=jnp.float32)
        parts = [
            scores[:, j * tile : (j + 1) * tile] + jnp.where(meta[r, bands + first + j] > 0, 0.0, MASKED)
            for j in range(window)
        ]
        more, far = picked(0, h, r)
        top, total, raised = softmax(parts + more)
        near = v_all[h][pl.ds(first, window)].reshape(window * tile, HEAD_DIM)
        near_sum[h][r] = jnp.dot(
            jnp.concatenate(raised[:window], axis=1), near, preferred_element_type=jnp.float32
        ) + jnp.dot(jnp.concatenate(raised[window:], axis=1), far, preferred_element_type=jnp.float32)
        near_top[h][r] = jnp.broadcast_to(top, (tile, HEAD_DIM))
        near_total[h][r] = jnp.broadcast_to(total, (tile, HEAD_DIM))

    def attend_far(h, r):
        parts, far = picked(1, h, r)
        before = near_top[h][r][:, :1]
        top, total, raised = softmax(parts, before)
        kept = jnp.exp2((before - top) * scale)
        total = near_total[h][r][:, :1] * kept + total
        result = jnp.dot(jnp.concatenate(raised, axis=1), far, preferred_element_type=jnp.float32)
        o_all[h][r] = ((near_sum[h][r] * kept + result) / total).astype(o_all[h].dtype)

    def give_back(h, peer):
        return pltpu.make_async_remote_copy(
            src_ref=o_all[h].at[peer],
            dst_ref=out.at[:, head_columns(me, h)],
            send_sem=o_send.at[h],
            recv_sem=o_recv.at[h],
            device_id={"space": peer},
            device_id_type=MESH,
        )

    def keep(h):
        return pltpu.make_async_copy(o_all[h].at[me], out.at[:, head_columns(me, h)], o_own.at[h])

    def near_loop(h):
        wait_spread(2, h)
        halo(0, h).wait_recv()

        @pl.loop(0, bands, unroll=2)
        def _(r):
            attend_near(h, r)

    def far_loop(h):
        @pl.when(exists[1])
        def _():
            halo(1, h).wait_recv()

        @pl.loop(0, bands // 2)
        def _(i):
            places = [place(2 * i + j) for j in range(2)]
            for r in places:
                attend_far(h, r)

            @pl.when(i != bands // 4)
            def _():
                give_back(h, places[0]).start()

            give_back(h, places[1]).start()

        keep(h).start()

    sent(0, 0)
    sent(1, 0)
    sent(0, 1)
    sent(1, 1)
    start_spread((2,), 0)
    fill_halo(0)
    start_spread((2,), 1)
    fill_halo(1)
    near_loop(0)
    near_loop(1)
    far_loop(0)
    far_loop(1)
    sent(2, 0)
    sent(2, 1)

    for h in range(heads):
        for side in range(2):
            @pl.when(exists[side])
            def _():
                halo(side, h).wait_send()
                if h == 0:
                    ask(side).wait_send()
        wait_bytes(o_all[h], o_send.at[h])
        wait_bytes(o_all[h], o_recv.at[h])
        keep(h).wait()


def body(queries, keys, values, tile_mask):
    bands = lax.axis_size("space")
    groups = lax.axis_size("tm")
    tile, width = queries.shape
    heads = width // HEAD_DIM // bands
    whole = (bands, tile, HEAD_DIM)
    halo = (2, UMAX, tile, HEAD_DIM)
    dma = pltpu.SemaphoreType.DMA
    return pl.pallas_call(
        functools.partial(kernel, bands, groups, heads),
        out_shape=pltpu.VMEM((tile, width), jnp.bfloat16),
        in_specs=[pl.BlockSpec(memory_space=pltpu.HBM)] * 4,
        out_specs=pl.BlockSpec(memory_space=pl.ANY),
        scratch_shapes=[pltpu.VMEM(whole, jnp.bfloat16)] * (4 * heads)
        + [pltpu.VMEM(halo, jnp.bfloat16)] * (4 * heads)
        + [pltpu.VMEM(whole, jnp.float32)] * (3 * heads)
        + [
            pltpu.VMEM(tile_mask.shape, jnp.int32),
            pltpu.VMEM((bands, LANES), jnp.int32),
            pltpu.SMEM((bands, LANES), jnp.int32),
            [pltpu.VMEM((8, LANES), jnp.int32)] * 2,
            [pltpu.VMEM((8, LANES), jnp.int32)] * 2,
            [pltpu.SMEM((8, LANES), jnp.int32)] * 2,
            dma,
            dma,
            dma((2,)),
            dma((2,)),
            dma((2,)),
            dma((3, heads)),
            dma((3, heads)),
            dma((3, heads)),
            dma((2, heads)),
            dma((2, heads)),
            dma((heads,)),
            dma((heads,)),
            dma((heads,)),
        ],
        compiler_params=pltpu.CompilerParams(
            collective_id=0, has_side_effects=True, vmem_limit_bytes=56 * 1024 * 1024
        ),
    )(tile_mask, queries, keys, values)


def solution(mesh):
    placed = (
        P(("tm", "space"), None),
        P(("tm", "space"), None),
        P(("tm", "space"), None),
        P("tm", None),
    )
    return jax.shard_map(
        body, mesh=mesh, in_specs=placed, out_specs=P(("tm", "space"), None), check_vma=False
    )
```
